32 devices in a mesh: dp: 16 (over z, y, x), group: 2 (over core).
Axes of the slice: x: 2, y: 2, z: 4, core: 2. Of those that a mesh axis runs over, the one named last changes fastest.
Arguments:
- embeddings: bfloat16 [32768, 1024], P('dp', 'group'), may hold values from -6 to 6
- assignment: int32 [32768], P('dp'), may hold values from -1 to 65535, as said below
- prev_counts: int32 [65536], P('dp'), may hold values from 1 to 8
- old_centroids: float32 [65536, 1024], P('dp', 'group'), may hold values from -4 to 4
- block_owner: int32 [1024], replicated, may hold values from 0 to 15, as said below
Outputs:
- new_centroids: float32 [65536, 1024], P('dp', 'group')
- max_sim: float32 [32768], P('dp')
The draws below stay inside these ranges and needn't reach their ends.
Inputs may be any that keep to these rules, and one draw needn't show every extreme that they name: `block_owner`: every owner owns exactly 64 blocks. `assignment`: -1 marks a padding document. On each index of dp, at most 256 documents belong to clusters of blocks owned by one index of dp, and some owner receives exactly 256 from every index of dp.
All inputs are finite; a program needn't handle non-finite values.
Results may differ from the reference program's by a relative error of at most 0.0003.
Values may be sent and summed in bfloat16 or wider, within the bound.
A program may use at most 128 MiB of HBM per device.

```python
import jax
import jax.numpy as jnp
from jax import lax

D = 1024
K = 65536
CB = 64
DOC_DEV = 2048
DOCS = 32768
CAP = 256
SLOTS = 4096
NBLK = 1024
BPO = 64
CPO = 4096


def owner_table(key):
    order = jax.random.permutation(jax.random.fold_in(key, 11), NBLK)
    return (order // BPO).astype(jnp.int32)


def draw_block_owner(key, part):
    return owner_table(key)


def draw_assignment(key, part):
    owner = owner_table(key)
    n_dp = SLOTS // CAP
    grouped = jnp.argsort(owner, stable=True).astype(jnp.int32).reshape(n_dp, BPO)
    full_owner = owner[NBLK - 1]

    def one_device(device):
        dkey = jax.random.fold_in(jax.random.fold_in(key, 17), device)
        keys = jax.random.split(dkey, 6)
        shuffled = jax.random.permutation(keys[0], SLOTS)
        slot_ids = jnp.arange(SLOTS, dtype=jnp.int32)
        scores = shuffled + jnp.where(slot_ids // CAP == full_owner, 0, SLOTS)
        taken = jnp.argsort(scores)[:DOC_DEV].astype(jnp.int32)
        dest = taken // CAP
        position = jnp.arange(DOC_DEV, dtype=jnp.int32)
        padding = jax.random.randint(keys[1], (DOC_DEV,), 0, 8) == 0
        padding = padding & (position >= CAP) | (position == DOC_DEV - 1)
        upper = jax.random.randint(keys[2], (DOC_DEV,), 1, CPO + 1)
        middle = jax.random.randint(keys[3], (DOC_DEV,), 1, upper + 1)
        local = jax.random.randint(keys[4], (DOC_DEV,), 0, middle)
        local = jnp.where(position == 0, CPO - 1, local)
        block = grouped[dest, local // CB]
        cluster = jnp.where(padding, -1, block * CB + local % CB)
        rows = jax.random.permutation(keys[5], DOC_DEV)
        return cluster[rows]
    return jax.vmap(one_device)(jnp.arange(n_dp)).reshape(-1).astype(jnp.int32)


def set_ends(result, rng, low, largest):
    spot = [jax.random.randint(jax.random.fold_in(rng, axis), (), 0, length) for axis, length in enumerate(result.shape)]
    longest = result.shape.index(max(result.shape))
    next_to = spot[:longest] + [(spot[longest] + 1) % result.shape[longest]] + spot[longest + 1:]
    return result.at[tuple(spot)].set(low).at[tuple(next_to)].set(largest)


def levels(rng, shape, cuts, low, high):
    def one(axis_at, blocks):
        heights = jax.random.uniform(jax.random.fold_in(jax.random.fold_in(rng, 6), axis_at), (blocks,), jnp.float32, low / len(cuts), high / len(cuts))
        return jnp.repeat(jnp.exp(heights), shape[axis_at] // blocks).reshape((-1,) + (1,) * (len(shape) - axis_at - 1))

    level = one(*cuts[0])
    for cut in cuts[1:]:
        level = level * one(*cut)
    return level


def gaussian(stream_key, dims, scale, most, cuts=(), kind=jnp.bfloat16):
    result = scale * jax.random.normal(stream_key, dims, jnp.float32)
    if cuts:
        result = result * levels(stream_key, dims, cuts, -0.22, 0.18)
    return jnp.clip(result, -most, most).astype(kind)


def setup_inputs(seed: int = 0) -> dict:
    streams_of = jax.random.split(jax.random.key(seed), 6)
    embeddings = gaussian(streams_of[0], (DOCS, D), 1.0, 6.0, ((0, 16), (1, 2)))
    assignment = draw_assignment(jax.random.fold_in(streams_of[5], 71), 0)
    prev_counts = set_ends(jax.random.randint(streams_of[2], (K,), 1, 9), jax.random.fold_in(streams_of[2], 1), 1, 8).astype(jnp.int32)
    old_centroids = gaussian(streams_of[3], (K, D), 0.5, 4.0, ((0, 16), (1, 2)), jnp.float32)
    block_owner = draw_block_owner(jax.random.fold_in(streams_of[5], 71), 0)
    return {"embeddings": embeddings, "assignment": assignment, "prev_counts": prev_counts, "old_centroids": old_centroids, "block_owner": block_owner}


def layout_clusters(block_owner):
    order = jnp.argsort(block_owner, stable=True).astype(jnp.int32)
    rows = jnp.arange(K, dtype=jnp.int32)
    return order[rows // CB] * CB + rows % CB

def reference(embeddings, assignment, prev_counts, old_centroids, block_owner):
    n_dp = DOCS // DOC_DEV
    valid = assignment >= 0
    safe = jnp.maximum(assignment, 0)
    wide = jnp.where(valid[:, None], embeddings.astype(jnp.float32), jnp.float32(0.0))
    sums = jax.ops.segment_sum(wide, safe, num_segments=K)
    counts = jax.ops.segment_sum(valid.astype(jnp.float32), safe, num_segments=K)
    layout = layout_clusters(block_owner)
    prev = prev_counts.astype(jnp.float32)
    new_centroids = (prev[:, None] * old_centroids + sums[layout]) / (prev + counts[layout])[:, None]
    inverse = lax.rsqrt(lax.optimization_barrier(jnp.sum(jnp.square(embeddings.astype(jnp.float32)), axis=1)) + 1e-06)
    dest = jnp.where(valid, block_owner[safe // CB], n_dp).astype(jnp.int32)
    order = jnp.argsort(dest, stable=True).astype(jnp.int32)
    sorted_dest = dest[order]
    per_owner = jax.ops.segment_sum(jnp.ones((DOCS,), jnp.int32), dest, num_segments=n_dp + 1)
    offsets = jnp.cumsum(per_owner) - per_owner
    within = jnp.arange(DOCS, dtype=jnp.int32) - offsets[sorted_dest]
    table = jnp.full((n_dp + 1, SLOTS), DOCS, jnp.int32).at[sorted_dest, within].set(order, mode='drop')[:n_dp]
    emb_pad = jnp.concatenate([embeddings, jnp.zeros((1, D), embeddings.dtype)], axis=0)
    ids_pad = jnp.concatenate([assignment, jnp.full((1,), -1, jnp.int32)])
    inv_pad = jnp.concatenate([inverse, jnp.ones((1,), jnp.float32)])
    eye = jnp.eye(SLOTS, dtype=bool)

    def owner_best(index_row):
        rows = emb_pad[index_row]
        ids = ids_pad[index_row]
        inv = inv_pad[index_row]
        gram = jnp.dot(rows, rows.T, preferred_element_type=jnp.float32)
        cosine = gram * inv[:, None] * inv[None, :]
        same = (ids[:, None] == ids[None, :]) & (ids[:, None] >= 0) & jnp.logical_not(eye)
        return lax.optimization_barrier(jnp.max(jnp.where(same, cosine, jnp.float32(-1.0)), axis=1))
    best = lax.map(owner_best, table)
    max_sim = jnp.full((DOCS + 1,), -1.0, jnp.float32).at[table.reshape(-1)].set(best.reshape(-1), mode='drop')[:DOCS]
    return (new_centroids, max_sim)
```

```python
import jax
import jax.numpy as jnp
from jax import lax
from jax.experimental import pallas as pl
from jax.experimental.pallas import tpu as pltpu
from jax.sharding import PartitionSpec as P

CB = 64
CHUNKS = 2
NEG = -3.0e38
BF = jnp.bfloat16


def gram_kernel(diagonal, own_ref, all_ref, pos_i, id_i, pos_j, id_j, inv_j, out_ref, best):
    j = pl.program_id(1)

    @pl.when(j == 0)
    def _():
        best[...] = jnp.full_like(best, NEG)

    gram = None
    for part in range(own_ref.shape[0]):
        term = lax.dot_general(
            own_ref[part], all_ref[part], (((1,), (1,)), ((), ())),
            preferred_element_type=jnp.float32,
        )
        gram = term if gram is None else gram + term
    same = pos_i[...] == pos_j[...]
    if diagonal:
        same = same & (id_i[...] != id_j[...])
    value = jnp.where(same, gram * inv_j[...], NEG)
    top = best[...]
    for lane in range(0, value.shape[1], 128):
        top = jnp.maximum(top, value[:, lane : lane + 128])
    best[...] = top

    @pl.when(j == pl.num_programs(1) - 1)
    def _():
        out_ref[...] = jnp.max(best[...], axis=1, keepdims=True)


def gram_best(diagonal, own, every, pos_i, id_i, pos_j, id_j, inv_j):
    parts, rows, half = own.shape
    cols = every.shape[1]
    ti, tj = min(512, rows), min(512, cols)
    column = pl.BlockSpec((ti, 1), lambda i, j: (i, 0))
    line = pl.BlockSpec((1, tj), lambda i, j: (0, j))
    out = pl.pallas_call(
        lambda *refs: gram_kernel(diagonal, *refs),
        grid=(rows // ti, cols // tj),
        in_specs=[
            pl.BlockSpec((parts, ti, half), lambda i, j: (0, i, 0)),
            pl.BlockSpec((parts, tj, half), lambda i, j: (0, j, 0)),
            column, column, line, line, line,
        ],
        out_specs=column,
        out_shape=jax.ShapeDtypeStruct((rows, 1), jnp.float32),
        scratch_shapes=[pltpu.VMEM((ti, 128), jnp.float32)],
        compiler_params=pltpu.CompilerParams(vmem_limit_bytes=32 * 1024 * 1024),
        cost_estimate=pl.CostEstimate(
            flops=2 * rows * cols * parts * half,
            bytes_accessed=2 * parts * half * (rows + cols * (rows // ti)),
            transcendentals=0,
        ),
    )(own, every, pos_i[:, None], id_i[:, None], pos_j[None, :], id_j[None, :], inv_j[None, :])
    return out[:, 0]


def before(n):
    index = jnp.arange(n, dtype=jnp.int32)
    return (index[None, :] < index[:, None]).astype(BF)


def dot(a, b):
    return jnp.dot(a, b, preferred_element_type=jnp.float32)


def on_device(embeddings, assignment, prev_counts, old_centroids, block_owner):
    n_dp = lax.axis_size("dp")
    n_grp = lax.axis_size("group")
    grp = lax.axis_index("group")
    doc_rows, half = embeddings.shape
    cap = 2 * doc_rows // n_dp
    owned = old_centroids.shape[0]
    n_blocks = block_owner.shape[0]
    width = cap // CHUNKS
    mine = width // n_grp
    part_rows = n_dp * width

    owners = jnp.arange(n_dp, dtype=jnp.int32)
    owner_hot = (block_owner[:, None] == owners[None, :]).astype(BF)
    rank = jnp.sum(dot(before(n_blocks), owner_hot) * owner_hot.astype(jnp.float32), axis=1)
    table = jnp.concatenate([owner_hot, (rank + 1.0).astype(BF)[:, None]], axis=1)
    block_hot = (
        (assignment >> 6)[:, None] == jnp.arange(n_blocks, dtype=jnp.int32)[None, :]
    ).astype(BF)
    look = dot(block_hot, table)
    dest_hot = look[:, :n_dp]
    dest_bf = dest_hot.astype(BF)
    valid = assignment >= 0
    order_in = jnp.sum(dot(before(doc_rows), dest_bf) * dest_hot, axis=1).astype(jnp.int32)
    dest = jnp.sum(dest_hot * owners.astype(jnp.float32)[None, :], axis=1).astype(jnp.int32)
    slot = jnp.where(valid, dest * cap + order_in, -1)
    order_hot = order_in[:, None] == jnp.arange(cap, dtype=jnp.int32)[None, :]
    low = (assignment & (CB - 1)).astype(jnp.float32)
    fields = jnp.concatenate(
        [
            jnp.where(order_hot, look[:, n_dp :], 0.0).astype(BF),
            jnp.where(order_hot, low[:, None], 0.0).astype(BF),
        ],
        axis=1,
    )
    meta = lax.dot_general(
        dest_bf, fields, (((0,), (0,)), ((), ())), preferred_element_type=jnp.float32
    ).astype(jnp.int32)
    places = (meta[:, :cap] - 1) * CB + meta[:, cap:]

    got_places = lax.all_to_all(places, "dp", split_axis=0, concat_axis=0, tiled=True)

    got = []
    for c in range(CHUNKS):
        names = (owners[:, None] * cap + c * width + jnp.arange(width, dtype=jnp.int32)).reshape(-1)
        pick = (names[:, None] == slot[None, :]).astype(BF)
        outgoing = dot(pick, embeddings).astype(BF).reshape(n_dp, width, half)
        got.append(lax.all_to_all(outgoing, "dp", split_axis=0, concat_axis=0, tiled=True))

    flat = got_places.reshape(-1)
    taken = flat >= 0
    block_in = jnp.arange(owned // CB, dtype=jnp.int32)
    hot_a = ((flat >> 6)[None, :] == block_in[:, None]) & taken[None, :]
    hot_b = (flat & (CB - 1))[:, None] == jnp.arange(CB, dtype=jnp.int32)[None, :]
    counts = dot(hot_a.astype(BF), hot_b.astype(BF)).reshape(-1)
    prev = prev_counts.astype(jnp.float32)
    total = prev[:, None] * old_centroids

    ids = jnp.arange(part_rows, dtype=jnp.int32)

    def own_part(x):
        axis = x.ndim - 2 if x.ndim > 2 else 1
        return lax.dynamic_slice_in_dim(x, grp * mine, mine, axis)

    chunks = []
    for c in range(CHUNKS):
        place = got_places[:, c * width : (c + 1) * width]
        line = place.reshape(-1)
        hot = (jnp.arange(owned, dtype=jnp.int32)[:, None] == line[None, :]).astype(BF)
        total = total + dot(hot, got[c].reshape(part_rows, half))
        every = lax.all_gather(got[c], "group", axis=0)
        own = own_part(every).reshape(n_grp, n_dp * mine, half)
        every = every.reshape(n_grp, part_rows, half)
        squares = jnp.sum(jnp.square(every.astype(jnp.float32)), axis=(0, 2))
        inverse = lax.rsqrt(squares + 1e-06)
        own_place = own_part(place).reshape(-1)
        chunks.append(
            dict(
                every=every, own=own, inverse=inverse,
                place_j=jnp.where(line >= 0, line, -2),
                place_i=jnp.where(own_place >= 0, own_place, -1),
                id_i=own_part(ids.reshape(n_dp, width)).reshape(-1),
                own_inverse=own_part(inverse.reshape(n_dp, width)).reshape(-1),
            )
        )
    best = []
    for a, left in enumerate(chunks):
        top = None
        for b, right in enumerate(chunks):
            value = gram_best(
                a == b, left["own"], right["every"], left["place_i"], left["id_i"],
                right["place_j"], ids, right["inverse"],
            )
            top = value if top is None else jnp.maximum(top, value)
        best.append(jnp.maximum(top * left["own_inverse"], -1.0).reshape(n_dp, 1, mine))
    best = jnp.concatenate(best, axis=1).reshape(n_dp, 1, CHUNKS * mine)
    spread = jnp.broadcast_to(best, (n_dp, n_grp, CHUNKS * mine)).reshape(n_dp * n_grp, -1)
    returned = lax.all_to_all(spread, ("dp", "group"), split_axis=0, concat_axis=0, tiled=True)
    returned = returned.reshape(n_dp, n_grp, CHUNKS, mine).transpose(0, 2, 1, 3).reshape(n_dp, cap)
    rows = jnp.dot(
        dest_hot, returned, precision=lax.Precision.HIGHEST, preferred_element_type=jnp.float32
    )
    max_sim = jnp.sum(jnp.where(order_hot, rows, 0.0), axis=1)
    max_sim = jnp.where(valid, max_sim, -1.0)
    new_centroids = total / (prev + counts)[:, None]
    return (new_centroids, max_sim)


def solution(mesh):
    return jax.shard_map(
        on_device,
        mesh=mesh,
        in_specs=(P("dp", "group"), P("dp"), P("dp"), P("dp", "group"), P()),
        out_specs=(P("dp", "group"), P("dp")),
        check_vma=False,
    )
```

```python
import jax
import jax.numpy as jnp
from jax import lax
from jax.experimental import pallas as pl
from jax.experimental.pallas import tpu as pltpu
from jax.sharding import PartitionSpec as P

CB = 64
EXTRA = 16
NEG = -3.0e38
BF = jnp.bfloat16


def gram_kernel(diagonal, own_ref, all_ref, key_i, key_j, inv_j, out_ref, best):
    j = pl.program_id(1)

    @pl.when(j == 0)
    def _():
        best[...] = jnp.full_like(best, NEG)

    gram = None
    for part in range(own_ref.shape[0]):
        term = lax.dot_general(
            own_ref[part], all_ref[part], (((1,), (1,)), ((), ())),
            preferred_element_type=jnp.float32,
        )
        gram = term if gram is None else gram + term
    same = key_i[:, 0:1] == key_j[0:1, :]
    if diagonal:
        same = same & (key_i[:, 1:2] != key_j[1:2, :])
    value = jnp.where(same, gram * inv_j[...], NEG)
    top = best[...]
    for lane in range(0, value.shape[1], 128):
        top = jnp.maximum(top, value[:, lane : lane + 128])
    best[...] = top

    @pl.when(j == pl.num_programs(1) - 1)
    def _():
        out_ref[...] = jnp.max(best[...], axis=1, keepdims=True)


def tile(size, step, most):
    return max([n for n in range(step, most + 1, step) if size % n == 0], default=size)


def gram_best(diagonal, own, every, key_i, key_j, inv_j):
    parts, rows, half = own.shape
    cols = every.shape[1]
    ti, tj = tile(rows, 16, 640), tile(cols, 128, 512)
    out = pl.pallas_call(
        lambda *refs: gram_kernel(diagonal, *refs),
        grid=(rows // ti, cols // tj),
        in_specs=[
            pl.BlockSpec((parts, ti, half), lambda i, j: (0, i, 0)),
            pl.BlockSpec((parts, tj, half), lambda i, j: (0, j, 0)),
            pl.BlockSpec((ti, 2), lambda i, j: (i, 0)),
            pl.BlockSpec((2, tj), lambda i, j: (0, j)),
            pl.BlockSpec((1, tj), lambda i, j: (0, j)),
        ],
        out_specs=pl.BlockSpec((ti, 1), lambda i, j: (i, 0)),
        out_shape=jax.ShapeDtypeStruct((rows, 1), jnp.float32),
        scratch_shapes=[pltpu.VMEM((ti, 128), jnp.float32)],
        compiler_params=pltpu.CompilerParams(vmem_limit_bytes=40 * 1024 * 1024),
        cost_estimate=pl.CostEstimate(
            flops=2 * rows * cols * parts * half,
            bytes_accessed=2 * parts * half * (rows + cols * (rows // ti)),
            transcendentals=0,
        ),
    )(own, every, key_i, key_j, inv_j[None, :])
    return out[:, 0]


def before(n):
    index = jnp.arange(n, dtype=jnp.int32)
    return (index[None, :] < index[:, None]).astype(BF)


def dot(a, b):
    return jnp.dot(a, b, preferred_element_type=jnp.float32)


def on_device(embeddings, assignment, prev_counts, old_centroids, block_owner):
    n_dp = lax.axis_size("dp")
    n_grp = lax.axis_size("group")
    grp = lax.axis_index("group")
    doc_rows, half = embeddings.shape
    cap = 2 * doc_rows // n_dp
    owned = old_centroids.shape[0]
    n_blocks = block_owner.shape[0]
    first = cap * 5 // 8
    starts, widths = (0, first), (first, cap - first)
    heights = (first + EXTRA, cap - first)

    owners = jnp.arange(n_dp, dtype=jnp.int32)
    owner_hot = (block_owner[:, None] == owners[None, :]).astype(BF)
    rank = jnp.sum(dot(before(n_blocks), owner_hot) * owner_hot.astype(jnp.float32), axis=1)
    table = jnp.concatenate([owner_hot, (rank + 1.0).astype(BF)[:, None]], axis=1)
    block_hot = (
        (assignment >> 6)[:, None] == jnp.arange(n_blocks, dtype=jnp.int32)[None, :]
    ).astype(BF)
    look = dot(block_hot, table)
    dest_hot = look[:, :n_dp]
    dest_bf = dest_hot.astype(BF)
    valid = assignment >= 0
    order_in = jnp.sum(dot(before(doc_rows), dest_bf) * dest_hot, axis=1).astype(jnp.int32)
    dest = jnp.sum(dest_hot * owners.astype(jnp.float32)[None, :], axis=1).astype(jnp.int32)
    slot = jnp.where(valid, dest * cap + order_in, -1)
    order_hot = order_in[:, None] == jnp.arange(cap, dtype=jnp.int32)[None, :]
    low = (assignment & (CB - 1)).astype(jnp.float32)
    fields = jnp.concatenate(
        [
            jnp.where(order_hot, look[:, n_dp :], 0.0).astype(BF),
            jnp.where(order_hot, low[:, None], 0.0).astype(BF),
        ],
        axis=1,
    )
    meta = lax.dot_general(
        dest_bf, fields, (((0,), (0,)), ((), ())), preferred_element_type=jnp.float32
    )
    meta = jnp.pad(meta, ((0, 0), (0, EXTRA * half - 2 * cap))).reshape(n_dp, EXTRA, half)
    meta = jnp.pad(meta, ((0, 0), (first, 0), (0, 0)))

    outgoing = []
    for c in range(2):
        row = jnp.arange(heights[c], dtype=jnp.int32)
        names = jnp.where(row < widths[c], owners[:, None] * cap + starts[c] + row, -2).reshape(-1)
        pick = (names[:, None] == slot[None, :]).astype(BF)
        rows = dot(pick, embeddings).reshape(n_dp, heights[c], half)
        outgoing.append((rows if c else rows + meta).astype(BF))
    early = lax.all_to_all(outgoing[0], "dp", split_axis=0, concat_axis=0, tiled=True)
    early, later = lax.optimization_barrier((early, outgoing[1]))
    got = [early, lax.all_to_all(later, "dp", split_axis=0, concat_axis=0, tiled=True)]
    fields = got[0][:, first:].reshape(n_dp, -1).astype(jnp.float32).astype(jnp.int32)
    got_places = (fields[:, :cap] - 1) * CB + fields[:, cap : 2 * cap]

    flat = got_places.reshape(-1)
    taken = flat >= 0
    block_in = jnp.arange(owned // CB, dtype=jnp.int32)
    hot_a = ((flat >> 6)[None, :] == block_in[:, None]) & taken[None, :]
    hot_b = (flat & (CB - 1))[:, None] == jnp.arange(CB, dtype=jnp.int32)[None, :]
    counts = dot(hot_a.astype(BF), hot_b.astype(BF)).reshape(-1)
    prev = prev_counts.astype(jnp.float32)
    total = prev[:, None] * old_centroids

    def gram_pair(left, right):
        return gram_best(
            left is right, left["own"], right["every"], left["key_i"], right["key_j"],
            right["inverse"],
        )

    chunks = []
    for c in range(2):
        if c:
            total, corner, got[c] = lax.optimization_barrier((total, corner, got[c]))
        mine, height = widths[c] // n_grp, heights[c]
        part_rows = n_dp * height

        def own_part(x, axis):
            return lax.dynamic_slice_in_dim(x, grp * mine, mine, axis)

        place = got_places[:, starts[c] : starts[c] + widths[c]]
        place = jnp.pad(place, ((0, 0), (0, height - widths[c])), constant_values=-1)
        line = place.reshape(-1)
        hot = (jnp.arange(owned, dtype=jnp.int32)[:, None] == line[None, :]).astype(BF)
        total = total + dot(hot, got[c].reshape(part_rows, half))
        every = lax.all_gather(got[c], "group", axis=0)
        own = own_part(every, 2).reshape(n_grp, n_dp * mine, half)
        every = every.reshape(n_grp, part_rows, half)
        squares = jnp.sum(jnp.square(every.astype(jnp.float32)), axis=(0, 2))
        inverse = lax.rsqrt(squares + 1e-06)
        ids = jnp.arange(part_rows, dtype=jnp.int32)
        own_place = own_part(place, 1).reshape(-1)
        own_ids = own_part(ids.reshape(n_dp, height), 1).reshape(-1)
        chunks.append(
            dict(
                every=every, own=own, inverse=inverse,
                key_i=jnp.stack([jnp.where(own_place >= 0, own_place, -1), own_ids], axis=1),
                key_j=jnp.stack([jnp.where(line >= 0, line, -2), ids], axis=0),
                own_inverse=own_part(inverse.reshape(n_dp, height), 1).reshape(-1),
            )
        )
        if c == 0:
            corner = gram_pair(chunks[0], chunks[0])
    one, two = chunks
    tops = (
        jnp.maximum(corner, gram_pair(one, two)),
        jnp.maximum(gram_pair(two, one), gram_pair(two, two)),
    )
    best = [
        jnp.maximum(top * x["own_inverse"], -1.0).reshape(n_dp, -1) for top, x in zip(tops, chunks)
    ]
    best = jnp.concatenate(best, axis=1)
    spread = jnp.broadcast_to(best[:, None], (n_dp, n_grp, cap // n_grp)).reshape(n_dp * n_grp, -1)
    returned = lax.all_to_all(spread, ("dp", "group"), split_axis=0, concat_axis=0, tiled=True)
    returned = returned.reshape(n_dp, n_grp, cap // n_grp)
    cut = first // n_grp
    returned = jnp.concatenate(
        [returned[:, :, :cut].reshape(n_dp, -1), returned[:, :, cut:].reshape(n_dp, -1)], axis=1
    )
    rows = jnp.dot(
        dest_hot, returned, precision=lax.Precision.HIGHEST, preferred_element_type=jnp.float32
    )
    max_sim = jnp.sum(jnp.where(order_hot, rows, 0.0), axis=1)
    max_sim = jnp.where(valid, max_sim, -1.0)
    new_centroids = total / (prev + counts)[:, None]
    return (new_centroids, max_sim)


def solution(mesh):
    return jax.shard_map(
        on_device,
        mesh=mesh,
        in_specs=(P("dp", "group"), P("dp"), P("dp"), P("dp", "group"), P()),
        out_specs=(P("dp", "group"), P("dp")),
        check_vma=False,
    )
```

```python
import functools

import jax
import jax.numpy as jnp
from jax import lax
from jax.experimental import pallas as pl
from jax.experimental.pallas import tpu as pltpu
from jax.sharding import PartitionSpec as P

CB = 64
EXTRA = 16
NEG = -3.0e38
BF = jnp.bfloat16


def gram_kernel(diagonal, own_ref, all_ref, key_i, key_j, inv_j, out_ref, best):
    j = pl.program_id(1)

    @pl.when(j == 0)
    def _():
        best[...] = jnp.full_like(best, NEG)

    gram = None
    for part in range(own_ref.shape[0]):
        term = lax.dot_general(
            own_ref[part], all_ref[part], (((1,), (1,)), ((), ())),
            preferred_element_type=jnp.float32,
        )
        gram = term if gram is None else gram + term
    same = key_i[:, 0:1] == key_j[0:1, :]
    if diagonal:
        same = same & (key_i[:, 1:2] != key_j[1:2, :])
    value = jnp.where(same, gram * inv_j[...], NEG)
    top = best[...]
    for lane in range(0, value.shape[1], 128):
        top = jnp.maximum(top, value[:, lane : lane + 128])
    best[...] = top

    @pl.when(j == pl.num_programs(1) - 1)
    def _():
        out_ref[...] = jnp.max(best[...], axis=1, keepdims=True)


def tile(size, step, most):
    return max([n for n in range(step, most + 1, step) if size % n == 0], default=size)


def gram_best(diagonal, own, every, key_i, key_j, inv_j):
    parts, rows, half = own.shape
    cols = every.shape[1]
    ti, tj = tile(rows, 16, 768), tile(cols, 128, 768)
    out = pl.pallas_call(
        lambda *refs: gram_kernel(diagonal, *refs),
        grid=(rows // ti, cols // tj),
        in_specs=[
            pl.BlockSpec((parts, ti, half), lambda i, j: (0, i, 0)),
            pl.BlockSpec((parts, tj, half), lambda i, j: (0, j, 0)),
            pl.BlockSpec((ti, 2), lambda i, j: (i, 0)),
            pl.BlockSpec((2, tj), lambda i, j: (0, j)),
            pl.BlockSpec((1, tj), lambda i, j: (0, j)),
        ],
        out_specs=pl.BlockSpec((ti, 1), lambda i, j: (i, 0)),
        out_shape=jax.ShapeDtypeStruct((rows, 1), jnp.float32),
        scratch_shapes=[pltpu.VMEM((ti, 128), jnp.float32)],
        compiler_params=pltpu.CompilerParams(vmem_limit_bytes=56 * 1024 * 1024),
        cost_estimate=pl.CostEstimate(
            flops=2 * rows * cols * parts * half,
            bytes_accessed=2 * parts * half * (rows + cols * (rows // ti)),
            transcendentals=0,
        ),
    )(own, every, key_i, key_j, inv_j[None, :])
    return out[:, 0]


def before(n):
    index = jnp.arange(n, dtype=jnp.int32)
    return (index[None, :] < index[:, None]).astype(BF)


def dot(a, b):
    return jnp.dot(a, b, preferred_element_type=jnp.float32)


def on_device(embeddings, assignment, prev_counts, old_centroids, block_owner):
    n_dp = lax.axis_size("dp")
    n_grp = lax.axis_size("group")
    grp = lax.axis_index("group")
    doc_rows, half = embeddings.shape
    cap = 2 * doc_rows // n_dp
    owned = old_centroids.shape[0]
    n_blocks = block_owner.shape[0]
    first = -(-(cap * 5 // 16) // n_grp) * n_grp
    second = cap * 3 // 8
    starts = (0, first, first + second)
    widths = (first, second, cap - first - second)
    heights = (first + EXTRA,) + widths[1:]

    owners = jnp.arange(n_dp, dtype=jnp.int32)
    owner_hot = (block_owner[:, None] == owners[None, :]).astype(BF)
    rank = jnp.sum(dot(before(n_blocks), owner_hot) * owner_hot.astype(jnp.float32), axis=1)
    table = jnp.concatenate([owner_hot, (rank + 1.0).astype(BF)[:, None]], axis=1)
    block_hot = (
        (assignment >> 6)[:, None] == jnp.arange(n_blocks, dtype=jnp.int32)[None, :]
    ).astype(BF)
    look = dot(block_hot, table)
    dest_hot = look[:, :n_dp]
    dest_bf = dest_hot.astype(BF)
    valid = assignment >= 0
    order_in = jnp.sum(dot(before(doc_rows), dest_bf) * dest_hot, axis=1).astype(jnp.int32)
    dest = jnp.sum(dest_hot * owners.astype(jnp.float32)[None, :], axis=1).astype(jnp.int32)
    slot = jnp.where(valid, dest * cap + order_in, -1)
    order_hot = order_in[:, None] == jnp.arange(cap, dtype=jnp.int32)[None, :]
    low = (assignment & (CB - 1)).astype(jnp.float32)
    fields = jnp.concatenate(
        [
            jnp.where(order_hot, look[:, n_dp :], 0.0).astype(BF),
            jnp.where(order_hot, low[:, None], 0.0).astype(BF),
        ],
        axis=1,
    )
    meta = lax.dot_general(
        dest_bf, fields, (((0,), (0,)), ((), ())), preferred_element_type=jnp.float32
    )
    meta = jnp.pad(meta, ((0, 0), (0, EXTRA * half - 2 * cap))).reshape(n_dp, EXTRA, half)
    meta = jnp.pad(meta, ((0, 0), (first, 0), (0, 0)))

    outgoing = []
    for c in range(3):
        row = jnp.arange(heights[c], dtype=jnp.int32)
        names = jnp.where(row < widths[c], owners[:, None] * cap + starts[c] + row, -2).reshape(-1)
        pick = (names[:, None] == slot[None, :]).astype(BF)
        rows = dot(pick, embeddings).reshape(n_dp, heights[c], half)
        outgoing.append((rows if c else rows + meta).astype(BF))
    got = []
    for c in range(3):
        rows = outgoing[c]
        if c:
            got[-1], rows = lax.optimization_barrier((got[-1], rows))
        got.append(lax.all_to_all(rows, "dp", split_axis=0, concat_axis=0, tiled=True))
    fields = got[0][:, first:].reshape(n_dp, -1).astype(jnp.float32).astype(jnp.int32)
    got_places = (fields[:, :cap] - 1) * CB + fields[:, cap : 2 * cap]

    flat = got_places.reshape(-1)
    taken = flat >= 0
    block_in = jnp.arange(owned // CB, dtype=jnp.int32)
    hot_a = ((flat >> 6)[None, :] == block_in[:, None]) & taken[None, :]
    hot_b = (flat & (CB - 1))[:, None] == jnp.arange(CB, dtype=jnp.int32)[None, :]
    counts = dot(hot_a.astype(BF), hot_b.astype(BF)).reshape(-1)
    prev = prev_counts.astype(jnp.float32)
    total = prev[:, None] * old_centroids

    def gram_pair(left, right):
        return gram_best(
            left is right, left["own"], right["every"], left["key_i"], right["key_j"],
            right["inverse"],
        )

    chunks, tops = [], []
    for c in range(3):
        if c:
            total, tops, got[c] = lax.optimization_barrier((total, tops, got[c]))
        mine, height = widths[c] // n_grp, heights[c]
        part_rows = n_dp * height

        def own_part(x, axis):
            return lax.dynamic_slice_in_dim(x, grp * mine, mine, axis)

        place = got_places[:, starts[c] : starts[c] + widths[c]]
        place = jnp.pad(place, ((0, 0), (0, height - widths[c])), constant_values=-1)
        line = place.reshape(-1)
        hot = (jnp.arange(owned, dtype=jnp.int32)[:, None] == line[None, :]).astype(BF)
        total = total + dot(hot, got[c].reshape(part_rows, half))
        every = lax.all_gather(got[c], "group", axis=0)
        if c == 2:
            total = total / (prev + counts)[:, None]
        total, every = lax.optimization_barrier((total, every))
        own = own_part(every, 2).reshape(n_grp, n_dp * mine, half)
        every = every.reshape(n_grp, part_rows, half)
        squares = jnp.sum(jnp.square(every.astype(jnp.float32)), axis=(0, 2))
        inverse = lax.rsqrt(squares + 1e-06)
        ids = jnp.arange(part_rows, dtype=jnp.int32)
        own_place = own_part(place, 1).reshape(-1)
        own_ids = own_part(ids.reshape(n_dp, height), 1).reshape(-1)
        chunks.append(
            dict(
                every=every, own=own, inverse=inverse,
                key_i=jnp.stack([jnp.where(own_place >= 0, own_place, -1), own_ids], axis=1),
                key_j=jnp.stack([jnp.where(line >= 0, line, -2), ids], axis=0),
                own_inverse=own_part(inverse.reshape(n_dp, height), 1).reshape(-1),
            )
        )
        new = chunks[c]
        tops = [
            jnp.maximum(top, gram_pair(old, new)) for top, old in zip(tops, chunks)
        ] + [functools.reduce(jnp.maximum, [gram_pair(new, old) for old in chunks])]
    best = [
        jnp.maximum(top * x["own_inverse"], -1.0).reshape(n_dp, -1) for top, x in zip(tops, chunks)
    ]
    best = jnp.concatenate(best, axis=1)
    spread = jnp.broadcast_to(best[:, None], (n_dp, n_grp, cap // n_grp)).reshape(n_dp * n_grp, -1)
    returned = lax.all_to_all(spread, ("dp", "group"), split_axis=0, concat_axis=0, tiled=True)
    returned = returned.reshape(n_dp, n_grp, cap // n_grp)
    cuts = [start // n_grp for start in starts] + [cap // n_grp]
    returned = jnp.concatenate(
        [returned[:, :, a:b].reshape(n_dp, -1) for a, b in zip(cuts, cuts[1:])], axis=1
    )
    rows = jnp.dot(
        dest_hot, returned, precision=lax.Precision.HIGHEST, preferred_element_type=jnp.float32
    )
    max_sim = jnp.sum(jnp.where(order_hot, rows, 0.0), axis=1)
    max_sim = jnp.where(valid, max_sim, -1.0)
    return (total, max_sim)


def solution(mesh):
    return jax.shard_map(
        on_device,
        mesh=mesh,
        in_specs=(P("dp", "group"), P("dp"), P("dp"), P("dp", "group"), P()),
        out_specs=(P("dp", "group"), P("dp")),
        check_vma=False,
    )
```

```python
import jax
import jax.numpy as jnp
from jax import lax
from jax.experimental import pallas as pl
from jax.experimental.pallas import tpu as pltpu
from jax.sharding import PartitionSpec as P

CB = 64
EXTRA = 16
NEG = -3.0e38
BF = jnp.bfloat16


def gram_kernel(diagonal, own_ref, all_ref, key_i, key_j, inv_j, out_ref, best):
    j = pl.program_id(1)

    @pl.when(j == 0)
    def _():
        best[...] = jnp.full_like(best, NEG)

    gram = None
    for part in range(own_ref.shape[0]):
        term = lax.dot_general(
            own_ref[part], all_ref[part], (((1,), (1,)), ((), ())),
            preferred_element_type=jnp.float32,
        )
        gram = term if gram is None else gram + term
    same = key_i[:, 0:1] == key_j[0:1, :]
    if diagonal:
        same = same & (key_i[:, 1:2] != key_j[1:2, :])
    value = jnp.where(same, gram * inv_j[...], NEG)
    top = best[...]
    for lane in range(0, value.shape[1], 128):
        top = jnp.maximum(top, value[:, lane : lane + 128])
    best[...] = top

    @pl.when(j == pl.num_programs(1) - 1)
    def _():
        out_ref[...] = jnp.max(best[...], axis=1, keepdims=True)


def tile(size, step, most):
    return max([n for n in range(step, most + 1, step) if size % n == 0], default=size)


def gram_best(diagonal, own, every, key_i, key_j, inv_j):
    parts, rows, half = own.shape
    cols = every.shape[1]
    ti, tj = tile(rows, 16, 448), tile(cols, 128, 512)
    out = pl.pallas_call(
        lambda *refs: gram_kernel(diagonal, *refs),
        grid=(rows // ti, cols // tj),
        in_specs=[
            pl.BlockSpec((parts, ti, half), lambda i, j: (0, i, 0)),
            pl.BlockSpec((parts, tj, half), lambda i, j: (0, j, 0)),
            pl.BlockSpec((ti, 2), lambda i, j: (i, 0)),
            pl.BlockSpec((2, tj), lambda i, j: (0, j)),
            pl.BlockSpec((1, tj), lambda i, j: (0, j)),
        ],
        out_specs=pl.BlockSpec((ti, 1), lambda i, j: (i, 0)),
        out_shape=jax.ShapeDtypeStruct((rows, 1), jnp.float32),
        scratch_shapes=[pltpu.VMEM((ti, 128), jnp.float32)],
        compiler_params=pltpu.CompilerParams(vmem_limit_bytes=56 * 1024 * 1024),
        cost_estimate=pl.CostEstimate(
            flops=2 * rows * cols * parts * half,
            bytes_accessed=2 * parts * half * (rows + cols * (rows // ti)),
            transcendentals=0,
        ),
    )(own, every, key_i, key_j, inv_j[None, :])
    return out[:, 0]


def before(n):
    index = jnp.arange(n, dtype=jnp.int32)
    return (index[None, :] < index[:, None]).astype(BF)


def dot(a, b):
    return jnp.dot(a, b, preferred_element_type=jnp.float32)


def on_device(embeddings, assignment, prev_counts, old_centroids, block_owner):
    n_dp = lax.axis_size("dp")
    n_grp = lax.axis_size("group")
    grp = lax.axis_index("group")
    doc_rows, half = embeddings.shape
    cap = 2 * doc_rows // n_dp
    owned = old_centroids.shape[0]
    n_blocks = block_owner.shape[0]
    first = -(-(cap * 7 // 16) // n_grp) * n_grp
    starts, widths = (0, first), (first, cap - first)
    heights = (first + EXTRA, cap - first)

    owners = jnp.arange(n_dp, dtype=jnp.int32)
    owner_hot = (block_owner[:, None] == owners[None, :]).astype(BF)
    rank = jnp.sum(dot(before(n_blocks), owner_hot) * owner_hot.astype(jnp.float32), axis=1)
    table = jnp.concatenate([owner_hot, (rank + 1.0).astype(BF)[:, None]], axis=1)
    block_hot = (
        (assignment >> 6)[:, None] == jnp.arange(n_blocks, dtype=jnp.int32)[None, :]
    ).astype(BF)
    look = dot(block_hot, table)
    dest_hot = look[:, :n_dp]
    dest_bf = dest_hot.astype(BF)
    valid = assignment >= 0
    order_in = jnp.sum(dot(before(doc_rows), dest_bf) * dest_hot, axis=1).astype(jnp.int32)
    dest = jnp.sum(dest_hot * owners.astype(jnp.float32)[None, :], axis=1).astype(jnp.int32)
    slot = jnp.where(valid, dest * cap + order_in, -1)
    order_hot = order_in[:, None] == jnp.arange(cap, dtype=jnp.int32)[None, :]
    low = (assignment & (CB - 1)).astype(jnp.float32)
    fields = jnp.concatenate(
        [
            jnp.where(order_hot, look[:, n_dp :], 0.0).astype(BF),
            jnp.where(order_hot, low[:, None], 0.0).astype(BF),
        ],
        axis=1,
    )
    meta = lax.dot_general(
        dest_bf, fields, (((0,), (0,)), ((), ())), preferred_element_type=jnp.float32
    )
    meta = jnp.pad(meta, ((0, 0), (0, EXTRA * half - 2 * cap))).reshape(n_dp, EXTRA, half)
    meta = jnp.pad(meta, ((0, 0), (first, 0), (0, 0)))

    outgoing = []
    for c in range(2):
        row = jnp.arange(heights[c], dtype=jnp.int32)
        names = jnp.where(row < widths[c], owners[:, None] * cap + starts[c] + row, -2).reshape(-1)
        pick = (names[:, None] == slot[None, :]).astype(BF)
        rows = dot(pick, embeddings).reshape(n_dp, heights[c], half)
        outgoing.append((rows if c else rows + meta).astype(BF))
    early = lax.all_to_all(outgoing[0], "dp", split_axis=0, concat_axis=0, tiled=True)
    early, later = lax.optimization_barrier((early, outgoing[1]))
    got = [early, lax.all_to_all(later, "dp", split_axis=0, concat_axis=0, tiled=True)]
    fields = got[0][:, first:].reshape(n_dp, -1).astype(jnp.float32).astype(jnp.int32)
    got_places = (fields[:, :cap] - 1) * CB + fields[:, cap : 2 * cap]

    flat = got_places.reshape(-1)
    taken = flat >= 0
    block_in = jnp.arange(owned // CB, dtype=jnp.int32)
    hot_a = ((flat >> 6)[None, :] == block_in[:, None]) & taken[None, :]
    hot_b = (flat & (CB - 1))[:, None] == jnp.arange(CB, dtype=jnp.int32)[None, :]
    counts = dot(hot_a.astype(BF), hot_b.astype(BF)).reshape(-1)
    prev = prev_counts.astype(jnp.float32)
    total = prev[:, None] * old_centroids

    def gram_pair(left, right):
        return gram_best(
            left is right, left["own"], right["every"], left["key_i"], right["key_j"],
            right["inverse"],
        )

    chunks = []
    for c in range(2):
        if c:
            total, corner, got[c] = lax.optimization_barrier((total, corner, got[c]))
        mine, height = widths[c] // n_grp, heights[c]
        part_rows = n_dp * height

        def own_part(x, axis):
            return lax.dynamic_slice_in_dim(x, grp * mine, mine, axis)

        place = got_places[:, starts[c] : starts[c] + widths[c]]
        place = jnp.pad(place, ((0, 0), (0, height - widths[c])), constant_values=-1)
        line = place.reshape(-1)
        hot = (jnp.arange(owned, dtype=jnp.int32)[:, None] == line[None, :]).astype(BF)
        total = total + dot(hot, got[c].reshape(part_rows, half))
        every = lax.all_gather(got[c], "group", axis=0)
        if c:
            total = total / (prev + counts)[:, None]
        total, every = lax.optimization_barrier((total, every))
        own = own_part(every, 2).reshape(n_grp, n_dp * mine, half)
        every = every.reshape(n_grp, part_rows, half)
        squares = jnp.sum(jnp.square(every.astype(jnp.float32)), axis=(0, 2))
        inverse = lax.rsqrt(squares + 1e-06)
        ids = jnp.arange(part_rows, dtype=jnp.int32)
        own_place = own_part(place, 1).reshape(-1)
        own_ids = own_part(ids.reshape(n_dp, height), 1).reshape(-1)
        chunks.append(
            dict(
                every=every, own=own, inverse=inverse,
                key_i=jnp.stack([jnp.where(own_place >= 0, own_place, -1), own_ids], axis=1),
                key_j=jnp.stack([jnp.where(line >= 0, line, -2), ids], axis=0),
                own_inverse=own_part(inverse.reshape(n_dp, height), 1).reshape(-1),
            )
        )
        if c == 0:
            corner = gram_pair(chunks[0], chunks[0])
    one, two = chunks
    tops = (
        jnp.maximum(corner, gram_pair(one, two)),
        jnp.maximum(gram_pair(two, one), gram_pair(two, two)),
    )
    best = [
        jnp.maximum(top * x["own_inverse"], -1.0).reshape(n_dp, -1) for top, x in zip(tops, chunks)
    ]
    best = jnp.concatenate(best, axis=1)
    spread = jnp.broadcast_to(best[:, None], (n_dp, n_grp, cap // n_grp)).reshape(n_dp * n_grp, -1)
    returned = lax.all_to_all(spread, ("dp", "group"), split_axis=0, concat_axis=0, tiled=True)
    returned = returned.reshape(n_dp, n_grp, cap // n_grp)
    cut = first // n_grp
    returned = jnp.concatenate(
        [returned[:, :, :cut].reshape(n_dp, -1), returned[:, :, cut:].reshape(n_dp, -1)], axis=1
    )
    rows = jnp.dot(
        dest_hot, returned, precision=lax.Precision.HIGHEST, preferred_element_type=jnp.float32
    )
    max_sim = jnp.sum(jnp.where(order_hot, rows, 0.0), axis=1)
    max_sim = jnp.where(valid, max_sim, -1.0)
    return (total, max_sim)


def solution(mesh):
    return jax.shard_map(
        on_device,
        mesh=mesh,
        in_specs=(P("dp", "group"), P("dp"), P("dp"), P("dp", "group"), P()),
        out_specs=(P("dp", "group"), P("dp")),
        check_vma=False,
    )
```

```python
import jax
import jax.numpy as jnp
from jax import lax
from jax.experimental import pallas as pl
from jax.experimental.pallas import tpu as pltpu
from jax.sharding import PartitionSpec as P

CB = 64
EXTRA = 16
NEG = -3.0e38
BF = jnp.bfloat16


def gram_kernel(diagonal, own_ref, all_ref, key_i, key_j, inv_j, out_ref, best):
    j = pl.program_id(1)

    @pl.when(j == 0)
    def _():
        best[...] = jnp.full_like(best, NEG)

    gram = None
    for part in range(own_ref.shape[0]):
        term = lax.dot_general(
            own_ref[part], all_ref[part], (((1,), (1,)), ((), ())),
            preferred_element_type=jnp.float32,
        )
        gram = term if gram is None else gram + term
    same = key_i[:, 0:1] == key_j[0:1, :]
    if diagonal:
        same = same & (key_i[:, 1:2] != key_j[1:2, :])
    value = jnp.where(same, gram * inv_j[...], NEG)
    top = best[...]
    for lane in range(0, value.shape[1], 128):
        top = jnp.maximum(top, value[:, lane : lane + 128])
    best[...] = top

    @pl.when(j == pl.num_programs(1) - 1)
    def _():
        out_ref[...] = jnp.max(best[...], axis=1, keepdims=True)


def tile(size, step, most):
    return max([n for n in range(step, most + 1, step) if size % n == 0], default=size)


def gram_best(diagonal, own, every, key_i, key_j, inv_j):
    parts, rows, half = own.shape
    cols = every.shape[1]
    ti, tj = tile(rows, 128, 640), tile(cols, 256, 512)
    out = pl.pallas_call(
        lambda *refs: gram_kernel(diagonal, *refs),
        grid=(rows // ti, cols // tj),
        in_specs=[
            pl.BlockSpec((parts, ti, half), lambda i, j: (0, i, 0)),
            pl.BlockSpec((parts, tj, half), lambda i, j: (0, j, 0)),
            pl.BlockSpec((ti, 2), lambda i, j: (i, 0)),
            pl.BlockSpec((2, tj), lambda i, j: (0, j)),
            pl.BlockSpec((1, tj), lambda i, j: (0, j)),
        ],
        out_specs=pl.BlockSpec((ti, 1), lambda i, j: (i, 0)),
        out_shape=jax.ShapeDtypeStruct((rows, 1), jnp.float32),
        scratch_shapes=[pltpu.VMEM((ti, 128), jnp.float32)],
        compiler_params=pltpu.CompilerParams(vmem_limit_bytes=min(56, 32 + 4 * parts) * 1024 * 1024),
        cost_estimate=pl.CostEstimate(
            flops=2 * rows * cols * parts * half,
            bytes_accessed=2 * parts * half * (rows + cols * (rows // ti)),
            transcendentals=0,
        ),
    )(own, every, key_i, key_j, inv_j[None, :])
    return out[:, 0]


def before(n):
    index = jnp.arange(n, dtype=jnp.int32)
    return (index[None, :] < index[:, None]).astype(BF)


def dot(a, b):
    return jnp.dot(a, b, preferred_element_type=jnp.float32)


def on_device(embeddings, assignment, prev_counts, old_centroids, block_owner):
    n_dp = lax.axis_size("dp")
    n_grp = lax.axis_size("group")
    grp = lax.axis_index("group")
    doc_rows, half = embeddings.shape
    cap = 2 * doc_rows // n_dp
    owned = old_centroids.shape[0]
    n_blocks = block_owner.shape[0]
    first = -(-(cap // 2) // n_grp) * n_grp
    starts, widths = (0, first), (first, cap - first)
    heights = (first + EXTRA, cap - first)

    owners = jnp.arange(n_dp, dtype=jnp.int32)
    owner_hot = (block_owner[:, None] == owners[None, :]).astype(BF)
    rank = jnp.sum(dot(before(n_blocks), owner_hot) * owner_hot.astype(jnp.float32), axis=1)
    table = jnp.concatenate([owner_hot, (rank + 1.0).astype(BF)[:, None]], axis=1)
    block_hot = (
        (assignment >> 6)[:, None] == jnp.arange(n_blocks, dtype=jnp.int32)[None, :]
    ).astype(BF)
    look = dot(block_hot, table)
    dest_hot = look[:, :n_dp]
    dest_bf = dest_hot.astype(BF)
    valid = assignment >= 0
    order_in = jnp.sum(dot(before(doc_rows), dest_bf) * dest_hot, axis=1).astype(jnp.int32)
    dest = jnp.sum(dest_hot * owners.astype(jnp.float32)[None, :], axis=1).astype(jnp.int32)
    slot = jnp.where(valid, dest * cap + order_in, -1)
    order_hot = order_in[:, None] == jnp.arange(cap, dtype=jnp.int32)[None, :]
    low = (assignment & (CB - 1)).astype(jnp.float32)
    fields = jnp.concatenate(
        [
            jnp.where(order_hot, look[:, n_dp :], 0.0).astype(BF),
            jnp.where(order_hot, low[:, None], 0.0).astype(BF),
        ],
        axis=1,
    )
    meta = lax.dot_general(
        dest_bf, fields, (((0,), (0,)), ((), ())), preferred_element_type=jnp.float32
    )
    meta = jnp.pad(meta, ((0, 0), (0, EXTRA * half - 2 * cap))).reshape(n_dp, EXTRA, half)
    meta = jnp.pad(meta, ((0, 0), (first, 0), (0, 0)))

    outgoing = []
    for c in range(2):
        row = jnp.arange(heights[c], dtype=jnp.int32)
        names = jnp.where(row < widths[c], owners[:, None] * cap + starts[c] + row, -2).reshape(-1)
        pick = (names[:, None] == slot[None, :]).astype(BF)
        rows = dot(pick, embeddings).reshape(n_dp, heights[c], half)
        outgoing.append((rows if c else rows + meta).astype(BF))
    early = lax.all_to_all(outgoing[0], "dp", split_axis=0, concat_axis=0, tiled=True)
    early, later = lax.optimization_barrier((early, outgoing[1]))
    got = [early, lax.all_to_all(later, "dp", split_axis=0, concat_axis=0, tiled=True)]
    fields = got[0][:, first:].reshape(n_dp, -1).astype(jnp.float32).astype(jnp.int32)
    got_places = (fields[:, :cap] - 1) * CB + fields[:, cap : 2 * cap]

    flat = got_places.reshape(-1)
    taken = flat >= 0
    block_in = jnp.arange(owned // CB, dtype=jnp.int32)
    hot_a = ((flat >> 6)[None, :] == block_in[:, None]) & taken[None, :]
    hot_b = (flat & (CB - 1))[:, None] == jnp.arange(CB, dtype=jnp.int32)[None, :]
    counts = dot(hot_a.astype(BF), hot_b.astype(BF)).reshape(-1)
    prev = prev_counts.astype(jnp.float32)
    total = prev[:, None] * old_centroids

    def gram_pair(left, right):
        return gram_best(
            left is right, left["own"], right["every"], left["key_i"], right["key_j"],
            right["inverse"],
        )

    chunks = []
    for c in range(2):
        if c:
            total, corner, got[c] = lax.optimization_barrier((total, corner, got[c]))
        mine, height = widths[c] // n_grp, heights[c]
        part_rows = n_dp * height

        def own_part(x, axis):
            return lax.dynamic_slice_in_dim(x, grp * mine, mine, axis)

        place = got_places[:, starts[c] : starts[c] + widths[c]]
        place = jnp.pad(place, ((0, 0), (0, height - widths[c])), constant_values=-1)
        line = place.reshape(-1)
        hot = (jnp.arange(owned, dtype=jnp.int32)[:, None] == line[None, :]).astype(BF)
        total = total + dot(hot, got[c].reshape(part_rows, half))
        every = lax.all_gather(got[c], "group", axis=0)
        if c:
            total = total / (prev + counts)[:, None]
        total, every = lax.optimization_barrier((total, every))
        own = own_part(every, 2).reshape(n_grp, n_dp * mine, half)
        every = every.reshape(n_grp, part_rows, half)
        squares = jnp.sum(jnp.square(every.astype(jnp.float32)), axis=(0, 2))
        inverse = lax.rsqrt(squares + 1e-06)
        ids = jnp.arange(part_rows, dtype=jnp.int32)
        own_place = own_part(place, 1).reshape(-1)
        own_ids = own_part(ids.reshape(n_dp, height), 1).reshape(-1)
        chunks.append(
            dict(
                every=every, own=own, inverse=inverse,
                key_i=jnp.stack([jnp.where(own_place >= 0, own_place, -1), own_ids], axis=1),
                key_j=jnp.stack([jnp.where(line >= 0, line, -2), ids], axis=0),
                own_inverse=own_part(inverse.reshape(n_dp, height), 1).reshape(-1),
            )
        )
        if c == 0:
            corner = gram_pair(chunks[0], chunks[0])
    one, two = chunks
    tops = (
        jnp.maximum(corner, gram_pair(one, two)),
        jnp.maximum(gram_pair(two, one), gram_pair(two, two)),
    )
    best = [
        jnp.maximum(top * x["own_inverse"], -1.0).reshape(n_dp, -1) for top, x in zip(tops, chunks)
    ]
    best = jnp.concatenate(best, axis=1)
    spread = jnp.broadcast_to(best[:, None], (n_dp, n_grp, cap // n_grp)).reshape(n_dp * n_grp, -1)
    returned = lax.all_to_all(spread, ("dp", "group"), split_axis=0, concat_axis=0, tiled=True)
    returned = returned.reshape(n_dp, n_grp, cap // n_grp)
    cut = first // n_grp
    returned = jnp.concatenate(
        [returned[:, :, :cut].reshape(n_dp, -1), returned[:, :, cut:].reshape(n_dp, -1)], axis=1
    )
    rows = jnp.dot(
        dest_hot, returned, precision=lax.Precision.HIGHEST, preferred_element_type=jnp.float32
    )
    max_sim = jnp.sum(jnp.where(order_hot, rows, 0.0), axis=1)
    max_sim = jnp.where(valid, max_sim, -1.0)
    return (total, max_sim)


def solution(mesh):
    return jax.shard_map(
        on_device,
        mesh=mesh,
        in_specs=(P("dp", "group"), P("dp"), P("dp"), P("dp", "group"), P()),
        out_specs=(P("dp", "group"), P("dp")),
        check_vma=False,
    )
```
